32 devices in a mesh: mem: 4 (over y, x), patch: 8 (over z, core).
Axes of the slice: x: 2, y: 2, z: 4, core: 2. Of those that a mesh axis runs over, the one named last changes fastest.
Arguments:
- prior: bfloat16 [80, 32, 32768], P('mem', 'patch'), may hold values from -6 to 6
- obs_prior: bfloat16 [4096, 80, 128], P(('mem', 'patch')), may hold values from -8 to 8
- obs_depart: bfloat16 [4096, 128], P(('mem', 'patch')), may hold values from -6 to 6
- obs_rinv: bfloat16 [4096, 128], P(('mem', 'patch')), may hold values from 0.25 to 2
- loc_class: int32 [4096, 128], P(('mem', 'patch')), may hold values from 0 to 15
- block_owner: int32 [4096, 1], P(('mem', 'patch')), may hold values from 0 to 31; in each aligned block of 128 rows (0 to 127, 128 to 255, ...) at most 8 rows name the same one
- block_patch: int32 [4096], P(('mem', 'patch')), may hold values from 0 to 15
Outputs:
- analysis: bfloat16 [80, 32, 32768], P('mem', 'patch')
The draws below stay inside these ranges and needn't reach their ends.
Inputs may be any that keep to these rules, and one draw needn't show every extreme that they name: `block_owner`: in each aligned block of 128 rows (the rows of one device) no device index appears more than 8 times, a bound that some block reaches.
All inputs are finite; a program needn't handle non-finite values.
Results may differ from the reference program's by a relative error of at most 0.012.
Values may be sent and summed in bfloat16 or wider, within the bound.
A program may use at most 384 MiB of HBM per device.

```python
import math
import jax
import jax.numpy as jnp
import numpy as np
from jax import lax

K = 80
NLF = 32
PC = 64
PD = 16
OBS = 128
NB_DEV = 128
ITERS = 10
CAP = 8
COLS = 32768
NBLK = 4096
DEVICES = 32


def draw_obs_prior(key, part):
    key = jax.random.fold_in(key, 11)
    subkeys = jax.random.split(key, 5)
    spread = jnp.exp(jax.random.uniform(subkeys[0], (NBLK, K, 1), jnp.float32, math.log(0.1), 0.0))
    noise = jax.random.normal(subkeys[1], (NBLK, K, OBS), jnp.float32)
    loading = 0.3 * jax.random.normal(subkeys[2], (NBLK, K, 1), jnp.float32)
    common = jax.random.normal(subkeys[3], (NBLK, 1, OBS), jnp.float32)
    shifts = 2.0 * jax.random.normal(subkeys[4], (NBLK, 1, OBS), jnp.float32)
    values = jnp.clip(shifts + spread * noise + loading * common, -8.0, 8.0)
    return values.astype(jnp.bfloat16)


def plant(entries, stream_key, low, high):
    longest = entries.shape.index(max(entries.shape))
    spots = []
    for shift in (0, 1):
        where = [jax.random.randint(jax.random.fold_in(stream_key, axis), (), 0, length) for axis, length in enumerate(entries.shape)]
        where[longest] = (where[longest] + shift) % entries.shape[longest]
        spots.append(tuple(where))
    return entries.at[spots[0]].set(low).at[spots[1]].set(high)


def level_of(key, shape, pieces, low, largest):
    factor_of = 1.0
    for dim, shards_of in pieces:
        draws = jax.random.uniform(jax.random.fold_in(jax.random.fold_in(key, 6), dim), (shards_of,), jnp.float32, low / len(pieces), largest / len(pieces))
        factor_of = factor_of * jnp.repeat(jnp.exp(draws), shape[dim] // shards_of).reshape((-1,) + (1,) * (len(shape) - 1 - dim))
    return factor_of


def shared_out(key, own, number, rows, number_of, top, reach, slope):
    order = jax.random.permutation(key, number_of)
    packed, usual = load_shares(number_of, rows * top, reach, slope, True), load_shares(number_of, rows * top, reach, slope, False)
    places = jnp.arange(number_of)

    def named(tallies, rotation):
        used = int((tallies > 0).sum())
        fixed = max(1, used // 4)
        shifted = fixed + (places - fixed + rotation * (used - fixed)) % max(1, number_of - fixed)
        return jnp.zeros((number_of,), jnp.int32).at[order[jnp.where(places < fixed, places, shifted)]].set(jnp.asarray(tallies, jnp.int32))

    tallies = jnp.where(number % 4 == 0, named(packed, number // 4), named(usual, number - number // 4 - 1))
    mixed = jax.random.permutation(jax.random.fold_in(own, 3), number_of)
    donor, receiver = mixed[0:number_of // 2 * 2:2], mixed[1:number_of // 2 * 2:2]
    room = jnp.minimum(tallies[donor] - 1, reach - tallies[receiver]) // 2
    room = jnp.where((donor == order[0]) | (receiver == order[0]) | (tallies[receiver] == 0), 0, jnp.maximum(room, 0))
    shifted = jax.random.randint(jax.random.fold_in(own, 4), (number_of // 2,), 0, 1 << 20) % (room + 1)
    tallies = tallies.at[donor].add(-shifted).at[receiver].add(shifted)
    items = jnp.searchsorted(jnp.cumsum(tallies), jnp.arange(rows * top), side="right").astype(jnp.int32)
    grid = items.reshape(top, rows).T
    grid = grid[jax.random.permutation(jax.random.fold_in(own, 1), rows)]
    rotation = jax.random.randint(jax.random.fold_in(own, 2), (rows, 1), 0, top)
    return jnp.take_along_axis(grid, (jnp.arange(top)[None, :] + rotation) % top, axis=1)


def load_shares(number_of, total, bound, slope, full):
    loads = [(1 << 20) // math.isqrt(standing ** slope) + 1 for standing in range(1, number_of + 1)]
    largest = bound if full else min(bound, max(-(-total // number_of), total * loads[0] // sum(loads)))
    least = 1 if total - largest >= number_of - 1 else 0
    holding, spare = [largest] + [least] * (number_of - 1), total - largest - least * (number_of - 1)
    while spare > 0:
        free = [i for i in range(1, number_of) if holding[i] < largest] or [i for i in range(1, number_of) if holding[i] < bound]
        pool, budget = sum([loads[i] for i in free]), spare
        for i in free:
            extra = min(bound - holding[i], max(1, budget * loads[i] // pool), spare)
            holding[i] = holding[i] + extra
            spare = spare - extra
    return np.array(holding)


def gaussian(key, dims, scale, bound, cuts=(), kind=jnp.bfloat16):
    values = jax.random.normal(key, dims, jnp.float32) * scale
    if len(cuts) > 0:
        values = level_of(key, dims, cuts, -0.22, 0.18) * values
    return jnp.clip(values, min=-bound, max=bound).astype(kind)


def setup_inputs(seed: int = 0) -> dict:
    key_list = jax.random.split(jax.random.key(seed), 8)
    prior = gaussian(key_list[0], (K, NLF, COLS), 1.0, 6.0, ((0, 4), (1, 8)))
    obs_prior = draw_obs_prior(jax.random.fold_in(key_list[7], 71), 0)
    obs_depart = gaussian(key_list[2], (NBLK, OBS), 1.0, 6.0, ((0, 32),))
    obs_rinv = jnp.clip(jnp.exp(math.log(2.0) - 2.0794415 * jax.random.uniform(key_list[3], (NBLK, OBS), jnp.float32) ** level_of(key_list[3], (NBLK, OBS), ((0, 32),), -0.2, 0.2)), 0.25, 2.0).astype(jnp.bfloat16)
    loc_class = plant(jax.random.randint(key_list[4], (NBLK, OBS), 0, 16), jax.random.fold_in(key_list[4], 1), 0, 15).astype(jnp.int32)
    block_owner_keys = jax.random.split(jax.random.fold_in(key_list[5], 1), NBLK // NB_DEV)
    block_owner_turns = jax.random.permutation(jax.random.fold_in(key_list[5], 3), NBLK // NB_DEV)
    block_owner = jax.vmap(lambda own, number: shared_out(jax.random.fold_in(key_list[5], 2), own, number, NB_DEV, DEVICES, 1, CAP, 2))(block_owner_keys, block_owner_turns).reshape((NBLK, 1))
    block_patch = plant(jax.random.randint(key_list[6], (NBLK,), 0, PD), jax.random.fold_in(key_list[6], 1), 0, PD - 1).astype(jnp.int32)
    return {"prior": prior, "obs_prior": obs_prior, "obs_depart": obs_depart, "obs_rinv": obs_rinv, "loc_class": loc_class, "block_owner": block_owner, "block_patch": block_patch}


def loc_weight(classes):
    taper = 1.0 - classes.astype(jnp.float32) * 0.0625
    return taper * taper

def block_terms(values, depart, rinv, classes):
    average = lax.optimization_barrier(jnp.sum(values.astype(jnp.float32), axis=1, keepdims=True)) / values.shape[1]
    deviation = (values.astype(jnp.float32) - average).astype(jnp.bfloat16)
    factor = loc_weight(classes) * rinv.astype(jnp.float32)
    scaled = (deviation.astype(jnp.float32) * factor[:, None, :]).astype(jnp.bfloat16)
    gram_blocks = jnp.einsum('bko,bjo->bkj', scaled.astype(jnp.float32), deviation.astype(jnp.float32))
    drive_vec = jnp.einsum('bko,bo->bk', scaled.astype(jnp.float32), depart.astype(jnp.float32))
    return (gram_blocks, drive_vec)

def batch_product(left, right):
    return jnp.einsum('pij,pjk->pik', left, right, precision=lax.Precision.HIGHEST)

def batch_apply(left, vector):
    return jnp.einsum('pij,pj->pi', left, vector, precision=lax.Precision.HIGHEST)

def analysis_weights(gram, drive_vec):
    members = gram.shape[1]
    identity = jnp.eye(members, dtype=jnp.float32)
    system = (members - 1.0) * identity + gram
    frobenius = jnp.sqrt(lax.optimization_barrier(jnp.sum(system * system, axis=(1, 2))))
    scaled_sys = system / frobenius[:, None, None]
    inverse_root = jnp.broadcast_to(identity, system.shape)
    for sweep_index in range(ITERS):
        correction = 1.5 * identity - 0.5 * batch_product(inverse_root, scaled_sys)
        scaled_sys = batch_product(scaled_sys, correction)
        inverse_root = batch_product(correction, inverse_root)
    root = inverse_root / jnp.sqrt(frobenius)[:, None, None]
    mean_weight = batch_apply(root, batch_apply(root, drive_vec))
    return (jnp.sqrt(members - 1.0) * root + mean_weight[:, :, None]).astype(jnp.bfloat16)

def apply_weights(fields, weights):
    average = lax.optimization_barrier(jnp.sum(fields.astype(jnp.float32), axis=0)) / fields.shape[0]
    deviation = (fields.astype(jnp.float32) - average).astype(jnp.bfloat16)
    mixed = jnp.einsum('kfpc,pkj->jfpc', deviation.astype(jnp.float32), weights.astype(jnp.float32))
    return (average + mixed).astype(jnp.bfloat16)

def reference(prior, obs_prior, obs_depart, obs_rinv, loc_class, block_owner, block_patch):
    patch_total = PD * DEVICES
    patch_index = (block_owner[:, 0] * PD + block_patch).astype(jnp.int32)

    def accumulate(totals, group_index):
        first = (group_index * NB_DEV).astype(jnp.int32)

        def take_rows(array):
            return lax.dynamic_slice_in_dim(array, first, NB_DEV, 0)
        gram_blocks, drive_vec = block_terms(take_rows(obs_prior), take_rows(obs_depart), take_rows(obs_rinv), take_rows(loc_class))
        targets = take_rows(patch_index)
        return ((totals[0] + jax.ops.segment_sum(gram_blocks, targets, patch_total), totals[1] + jax.ops.segment_sum(drive_vec, targets, patch_total)), None)
    start_totals = (jnp.zeros((patch_total, K, K), jnp.float32), jnp.zeros((patch_total, K), jnp.float32))
    (gram, drive_vec), unused = lax.scan(accumulate, start_totals, jnp.arange(DEVICES, dtype=jnp.int32))
    weights = analysis_weights(gram, drive_vec).reshape(DEVICES, PD, K, K)
    grouped = prior.reshape(K, NLF, DEVICES, PD, PC).transpose(2, 0, 1, 3, 4)

    def one_group(pair):
        return apply_weights(pair[0], pair[1])
    result = lax.map(one_group, (grouped, weights))
    return result.transpose(1, 2, 0, 3, 4).reshape(K, NLF, DEVICES * PD * PC)
```

```python
import functools
import jax
import jax.numpy as jnp
from jax import lax
from jax.experimental import pallas as pl
from jax.experimental.pallas import tpu as pltpu
from jax.sharding import PartitionSpec as P

PD = 16
ITERS = 10
LANES = 128
CHUNK = 512
MESH = pl.DeviceIdType.MESH


def batch_product(left, right):
    return jnp.einsum("pij,pjk->pik", left, right, precision=lax.Precision.HIGHEST)


def batch_apply(left, vector):
    return jnp.einsum("pij,pj->pi", left, vector, precision=lax.Precision.HIGHEST)


def analysis_weights(gram, drive_vec):
    members = gram.shape[1]
    identity = jnp.eye(members, dtype=jnp.float32)
    system = (members - 1.0) * identity + gram
    frobenius = jnp.sqrt(jnp.sum(system * system, axis=(1, 2)))
    scaled_sys = system / frobenius[:, None, None]
    inverse_root = jnp.broadcast_to(identity, system.shape)
    for sweep_index in range(ITERS):
        correction = 1.5 * identity - 0.5 * batch_product(inverse_root, scaled_sys)
        scaled_sys = batch_product(scaled_sys, correction)
        inverse_root = batch_product(correction, inverse_root)
    root = inverse_root / jnp.sqrt(frobenius)[:, None, None]
    mean_weight = batch_apply(root, batch_apply(root, drive_vec))
    return (jnp.sqrt(members - 1.0) * root + mean_weight[:, :, None]).astype(jnp.bfloat16)


def slot_positions(block_owner, devices, capacity):
    block_dest = block_owner[:, 0]
    onehot = (block_dest[:, None] == jnp.arange(devices, dtype=jnp.int32)[None, :]).astype(
        jnp.int32
    )
    position = jnp.sum(jnp.cumsum(onehot, axis=0) * onehot, axis=1) - 1
    return block_dest * capacity + position


def spread_kernel(index, blocks, slots, sem):
    count = blocks.shape[0]

    def copy(b):
        return pltpu.make_async_copy(blocks.at[b], slots.at[index[b]], sem.at[b])

    def start(b, carry):
        copy(b).start()
        return carry

    def finish(b, carry):
        copy(b).wait()
        return carry

    lax.fori_loop(0, count, start, 0)
    lax.fori_loop(0, count, finish, 0)


def spread_blocks(index, blocks, total):
    return pl.pallas_call(
        spread_kernel,
        out_shape=jax.ShapeDtypeStruct((total,) + blocks.shape[1:], blocks.dtype),
        in_specs=[pl.BlockSpec(memory_space=pltpu.SMEM), pl.BlockSpec(memory_space=pl.ANY)],
        out_specs=pl.BlockSpec(memory_space=pl.ANY),
        scratch_shapes=[pltpu.SemaphoreType.DMA((blocks.shape[0],))],
        name="spread_blocks",
    )(index, blocks)


def exchange_kernel(mems, patches, prior, slots, aux, fields, got_slots, got_aux,
                    slot_send, slot_recv, aux_send, aux_recv, col_send, col_recv, own_sem):
    my_mem, my_patch = lax.axis_index("mem"), lax.axis_index("patch")
    devices = mems * patches
    me = my_mem * patches + my_patch
    cols = fields.shape[-1]

    def partner(step):
        dest = lax.rem(me + step, devices)
        return dest, (dest // patches, lax.rem(dest, patches))

    barrier = pltpu.get_barrier_semaphore()

    def greet(step, carry):
        pl.semaphore_signal(barrier, inc=1, device_id=partner(step)[1], device_id_type=MESH)
        return carry

    lax.fori_loop(1, devices, greet, 0)
    pl.semaphore_wait(barrier, devices - 1)

    def slot_copies(step):
        dest, where = partner(step)
        return (
            pltpu.make_async_remote_copy(
                src_ref=slots.at[dest], dst_ref=got_slots.at[me],
                send_sem=slot_send.at[step], recv_sem=slot_recv.at[step],
                device_id=where, device_id_type=MESH),
            pltpu.make_async_remote_copy(
                src_ref=aux.at[dest], dst_ref=got_aux.at[me],
                send_sem=aux_send.at[step], recv_sem=aux_recv.at[step],
                device_id=where, device_id_type=MESH),
        )

    def col_copy(step):
        dest = lax.rem(my_mem + step, mems)
        first = pl.multiple_of(dest * cols, LANES)
        return pltpu.make_async_remote_copy(
            src_ref=prior.at[:, :, pl.ds(first, cols)], dst_ref=fields.at[my_mem],
            send_sem=col_send.at[step], recv_sem=col_recv.at[step],
            device_id=(dest, my_patch), device_id_type=MESH)

    def start(step, carry):
        for copy in slot_copies(step):
            copy.start()
        return carry

    def finish(step, carry):
        for copy in slot_copies(step):
            copy.wait()
        return carry

    lax.fori_loop(1, devices, start, 0)
    for step in range(1, mems):
        col_copy(step).start()
    mine = (
        pltpu.make_async_copy(slots.at[me], got_slots.at[me], own_sem.at[0]),
        pltpu.make_async_copy(aux.at[me], got_aux.at[me], own_sem.at[1]),
        pltpu.make_async_copy(
            prior.at[:, :, pl.ds(pl.multiple_of(my_mem * cols, LANES), cols)],
            fields.at[my_mem], own_sem.at[2]),
    )
    for copy in mine:
        copy.start()
    for copy in mine:
        copy.wait()
    lax.fori_loop(1, devices, finish, 0)
    for step in range(1, mems):
        col_copy(step).wait()


def exchange(prior, slots, aux, mems, patches):
    part, lf, all_cols = prior.shape
    devices = mems * patches
    dma = pltpu.SemaphoreType.DMA
    return pl.pallas_call(
        functools.partial(exchange_kernel, mems, patches),
        out_shape=(
            jax.ShapeDtypeStruct((mems, part, lf, all_cols // mems), jnp.bfloat16),
            jax.ShapeDtypeStruct(slots.shape, slots.dtype),
            jax.ShapeDtypeStruct(aux.shape, aux.dtype),
        ),
        in_specs=[pl.BlockSpec(memory_space=pl.ANY)] * 3,
        out_specs=(pl.BlockSpec(memory_space=pl.ANY),) * 3,
        scratch_shapes=[dma((devices,)), dma((devices,)), dma((devices,)), dma((devices,)),
                        dma((mems,)), dma((mems,)), dma((3,))],
        compiler_params=pltpu.CompilerParams(collective_id=0, has_side_effects=True),
        name="exchange",
    )(prior, slots, aux)


def apply_kernel(mems, chunks, fields, weights, out, wide, mixed, buf, send, recv, own):
    my_mem, my_patch = lax.axis_index("mem"), lax.axis_index("patch")
    step = pl.program_id(0)
    part, lf, chunk = fields.shape[1], fields.shape[2], fields.shape[3]
    members = mems * part
    tiles = chunk // LANES
    cols = chunk * chunks
    half = LANES // 2

    @pl.when(step == 0)
    def _():
        barrier = pltpu.get_barrier_semaphore()
        for other in range(1, mems):
            pl.semaphore_signal(barrier, inc=1,
                                device_id=(lax.rem(my_mem + other, mems), my_patch),
                                device_id_type=MESH)
        pl.semaphore_wait(barrier, mems - 1)

    def place(owner, at):
        return out.at[:, :, pl.ds(pl.multiple_of(owner * cols + at * chunk, LANES), chunk)]

    def outgoing(at, other):
        dest = lax.rem(my_mem + other, mems)
        return pltpu.make_async_remote_copy(
            src_ref=buf.at[lax.rem(at, 2), dest], dst_ref=place(my_mem, at),
            send_sem=send.at[lax.rem(at, 2), other], recv_sem=recv.at[at, other],
            device_id=(dest, my_patch), device_id_type=MESH)

    def local_copy(at):
        return pltpu.make_async_copy(buf.at[lax.rem(at, 2), my_mem], place(my_mem, at),
                                     own.at[lax.rem(at, 2)])

    def drain(at):
        for other in range(1, mems):
            outgoing(at, other).wait_send()
        local_copy(at).wait()

    @pl.when(step >= 2)
    def _():
        drain(step - 2)

    for k in range(members):
        row = fields[k // part, k % part].astype(jnp.float32)
        for t in range(tiles):
            wide[t, lf * k:lf * k + lf, :] = row[:, t * LANES:(t + 1) * LANES]
    lane = lax.broadcasted_iota(jnp.int32, (members, LANES), 1)
    for t in range(tiles):
        averages, devs = [], []
        for f in range(lf):
            x = wide[t, pl.ds(f, members, stride=lf), :]
            average = jnp.sum(x, axis=0, keepdims=True) / members
            averages.append(average)
            devs.append((x - average).astype(jnp.bfloat16))
        y = jnp.dot(weights[t], jnp.concatenate(devs, axis=1), preferred_element_type=jnp.float32)
        for f in range(lf):
            z = y[:, f * LANES:(f + 1) * LANES]
            mixed[t, pl.ds(f, members, stride=lf), :] = averages[f] + jnp.where(
                lane < half, z[:members], z[members:])
    slot = lax.rem(step, 2)
    for j in range(members):
        row = jnp.concatenate([mixed[t, lf * j:lf * j + lf, :] for t in range(tiles)], axis=1)
        buf[slot, j // part, j % part] = row.astype(jnp.bfloat16)
    for other in range(1, mems):
        outgoing(step, other).start()
    local_copy(step).start()

    @pl.when(step == chunks - 1)
    def _():
        if chunks > 1:
            drain(step - 1)
        drain(step)

        def arrive(at, carry):
            for other in range(1, mems):
                outgoing(at, other).wait_recv()
            return carry

        lax.fori_loop(0, chunks, arrive, 0)


def apply_return(fields, weights, mems):
    unused, part, lf, cols = fields.shape
    members = mems * part
    chunk = CHUNK
    chunks = cols // chunk
    tiles = chunk // LANES
    dma = pltpu.SemaphoreType.DMA
    return pl.pallas_call(
        functools.partial(apply_kernel, mems, chunks),
        grid=(chunks,),
        out_shape=jax.ShapeDtypeStruct((part, lf, cols * mems), jnp.bfloat16),
        in_specs=[
            pl.BlockSpec((mems, part, lf, chunk), lambda i: (0, 0, 0, i)),
            pl.BlockSpec((tiles, 2 * members, members), lambda i: (i, 0, 0)),
        ],
        out_specs=pl.BlockSpec(memory_space=pl.ANY),
        scratch_shapes=[
            pltpu.VMEM((tiles, members * lf, LANES), jnp.float32),
            pltpu.VMEM((tiles, members * lf, LANES), jnp.float32),
            pltpu.VMEM((2, mems, part, lf, chunk), jnp.bfloat16),
            dma((2, mems)), dma((chunks, mems)), dma((2,)),
        ],
        compiler_params=pltpu.CompilerParams(collective_id=1, has_side_effects=True,
                                             vmem_limit_bytes=32 * 1024 * 1024),
        name="apply_return",
    )(fields, weights)


def local(prior, obs_prior, obs_depart, obs_rinv, loc_class, block_owner, block_patch):
    mems = lax.axis_size("mem")
    patches = lax.axis_size("patch")
    devices = mems * patches
    block_count, members, obs_count = obs_prior.shape
    capacity = 2 * block_count // devices
    slot_index = slot_positions(block_owner, devices, capacity)
    total = devices * capacity
    taper = 1.0 - loc_class.astype(jnp.float32) * 0.0625
    taper = (taper * taper).astype(jnp.bfloat16)
    tag = jnp.broadcast_to((block_patch + 1).astype(jnp.bfloat16)[:, None], obs_depart.shape)
    packed = jnp.stack([obs_depart, obs_rinv, taper, tag], axis=1)
    place = (slot_index[None, :] == jnp.arange(total, dtype=jnp.int32)[:, None])
    aux = jnp.einsum("sb,bro->sro", place.astype(jnp.bfloat16), packed,
                     preferred_element_type=jnp.float32).astype(jnp.bfloat16)
    slots = spread_blocks(slot_index, obs_prior, total)
    fields, got_slots, got_aux = exchange(
        prior,
        slots.reshape(devices, capacity, members, obs_count),
        aux.reshape(devices, capacity, 4, obs_count),
        mems, patches)
    side = got_aux.reshape(total, 4, obs_count)
    values = got_slots.reshape(total, members, obs_count)
    values = jnp.where(side[:, 3:4, :] > 0, values, jnp.zeros((), jnp.bfloat16))
    depart = side[:, 0]
    factor = side[:, 1].astype(jnp.float32) * side[:, 2].astype(jnp.float32)
    patch_of = side[:, 3, 0].astype(jnp.float32)
    average = jnp.sum(values, axis=1, keepdims=True, dtype=jnp.float32) / members
    deviation = (values.astype(jnp.float32) - average).astype(jnp.bfloat16)
    scaled = (deviation.astype(jnp.float32) * factor[:, None, :]).astype(jnp.bfloat16)
    gram_blocks = jnp.einsum("bko,bjo->bkj", scaled, deviation, preferred_element_type=jnp.float32)
    drive_blocks = jnp.einsum("bko,bo->bk", scaled, depart, preferred_element_type=jnp.float32)
    select = (patch_of[:, None] == (jnp.arange(PD, dtype=jnp.float32) + 1.0)[None, :]).astype(
        jnp.float32)
    gram = jnp.einsum("sp,skj->pkj", select, gram_blocks, precision=lax.Precision.HIGHEST)
    drive = jnp.einsum("sp,sk->pk", select, drive_blocks, precision=lax.Precision.HIGHEST)
    weights = jnp.swapaxes(analysis_weights(gram, drive), 1, 2)
    gathered = lax.all_gather(weights, "patch", axis=0, tiled=True)
    gathered = gathered.reshape(patches * PD // 2, 2 * members, members)
    return apply_return(fields, gathered, mems)


def solution(mesh):
    return jax.shard_map(
        local,
        mesh=mesh,
        in_specs=(
            P("mem", "patch", None),
            P(("mem", "patch"), None, None),
            P(("mem", "patch"), None),
            P(("mem", "patch"), None),
            P(("mem", "patch"), None),
            P(("mem", "patch"), None),
            P(("mem", "patch")),
        ),
        out_specs=P("mem", "patch", None),
        check_vma=False,
    )
```

```python
import functools
import jax
import jax.numpy as jnp
from jax import lax
from jax.experimental import pallas as pl
from jax.experimental.pallas import tpu as pltpu
from jax.sharding import PartitionSpec as P

PD = 16
ITERS = 10
LANES = 128
CHUNK = 512
MESH = pl.DeviceIdType.MESH


def batch_product(left, right):
    return jnp.einsum("pij,pjk->pik", left, right, precision=lax.Precision.HIGHEST)


def batch_apply(left, vector):
    return jnp.einsum("pij,pj->pi", left, vector, precision=lax.Precision.HIGHEST)


def analysis_weights(gram, drive_vec):
    members = gram.shape[1]
    identity = jnp.eye(members, dtype=jnp.float32)
    system = (members - 1.0) * identity + gram
    frobenius = jnp.sqrt(jnp.sum(system * system, axis=(1, 2)))
    scaled_sys = system / frobenius[:, None, None]
    inverse_root = 1.5 * identity - 0.5 * scaled_sys
    scaled_sys = batch_product(scaled_sys, inverse_root)
    for sweep_index in range(1, ITERS):
        correction = 1.5 * identity - 0.5 * batch_product(inverse_root, scaled_sys)
        scaled_sys = batch_product(scaled_sys, correction)
        inverse_root = batch_product(correction, inverse_root)
    root = inverse_root / jnp.sqrt(frobenius)[:, None, None]
    mean_weight = batch_apply(root, batch_apply(root, drive_vec))
    return (jnp.sqrt(members - 1.0) * root + mean_weight[:, :, None]).astype(jnp.bfloat16)


def slot_positions(block_owner, devices, capacity):
    block_dest = block_owner[:, 0]
    onehot = (block_dest[:, None] == jnp.arange(devices, dtype=jnp.int32)[None, :]).astype(
        jnp.int32
    )
    position = jnp.sum(jnp.cumsum(onehot, axis=0) * onehot, axis=1) - 1
    return block_dest * capacity + position


def spread_kernel(index, blocks, slots):
    slots[...] = jnp.zeros_like(slots)

    def place(b, carry):
        slots[index[b]] = blocks[b]
        return carry

    lax.fori_loop(0, blocks.shape[0], place, 0)


def spread_blocks(index, blocks, total):
    return pl.pallas_call(
        spread_kernel,
        out_shape=jax.ShapeDtypeStruct((total,) + blocks.shape[1:], blocks.dtype),
        in_specs=[pl.BlockSpec(memory_space=pltpu.SMEM), pl.BlockSpec(memory_space=pltpu.VMEM)],
        out_specs=pl.BlockSpec(memory_space=pltpu.VMEM),
        compiler_params=pltpu.CompilerParams(vmem_limit_bytes=32 * 1024 * 1024),
        name="spread_blocks",
    )(index, blocks)


def gather_kernel(patches, mine, out, far_send, far_recv, near_send, near_recv, own_sem):
    my_mem, my_patch = lax.axis_index("mem"), lax.axis_index("patch")
    chips = patches // 2
    chip, core = my_patch // 2, lax.rem(my_patch, 2)
    sibling = (my_mem, chip * 2 + 1 - core)

    def peer(step):
        return lax.rem(chip + step, chips) * 2 + core

    barrier = pltpu.get_barrier_semaphore()
    pl.semaphore_signal(barrier, inc=1, device_id=sibling, device_id_type=MESH)
    for step in range(1, chips):
        pl.semaphore_signal(barrier, inc=1, device_id=(my_mem, peer(step)), device_id_type=MESH)
    pl.semaphore_wait(barrier, chips)

    def far(step):
        return pltpu.make_async_remote_copy(
            src_ref=mine, dst_ref=out.at[my_patch],
            send_sem=far_send.at[step], recv_sem=far_recv.at[step],
            device_id=(my_mem, peer(step)), device_id_type=MESH)

    def near(step):
        source = mine if step == 0 else out.at[peer(chips - step)]
        return pltpu.make_async_remote_copy(
            src_ref=source, dst_ref=out.at[peer(chips - step)],
            send_sem=near_send.at[step], recv_sem=near_recv.at[step],
            device_id=sibling, device_id_type=MESH)

    for step in range(1, chips):
        far(step).start()
    near(0).start()
    own = pltpu.make_async_copy(mine, out.at[my_patch], own_sem)
    own.start()
    for step in range(1, chips):
        far(step).wait_recv()
        near(step).start()
    own.wait()
    for step in range(1, chips):
        far(step).wait_send()
    for step in range(chips):
        near(step).wait()


def gather_weights(weights, patches):
    dma = pltpu.SemaphoreType.DMA
    chips = patches // 2
    return pl.pallas_call(
        functools.partial(gather_kernel, patches),
        out_shape=jax.ShapeDtypeStruct((patches,) + weights.shape, weights.dtype),
        in_specs=[pl.BlockSpec(memory_space=pltpu.VMEM)],
        out_specs=pl.BlockSpec(memory_space=pl.ANY),
        scratch_shapes=[dma((chips,)), dma((chips,)), dma((chips,)), dma((chips,)), dma(())],
        compiler_params=pltpu.CompilerParams(collective_id=2, has_side_effects=True),
        name="gather_weights",
    )(weights)


def exchange_kernel(mems, patches, prior, slots, aux, fields, got_slots, got_aux,
                    slot_send, slot_recv, aux_send, aux_recv, col_send, col_recv, own_sem):
    my_mem, my_patch = lax.axis_index("mem"), lax.axis_index("patch")
    devices = mems * patches
    me = my_mem * patches + my_patch
    cols = fields.shape[-1]

    def partner(step):
        dest = lax.rem(me + step, devices)
        return dest, (dest // patches, lax.rem(dest, patches))

    barrier = pltpu.get_barrier_semaphore()

    def greet(step, carry):
        pl.semaphore_signal(barrier, inc=1, device_id=partner(step)[1], device_id_type=MESH)
        return carry

    lax.fori_loop(1, devices, greet, 0)
    pl.semaphore_wait(barrier, devices - 1)

    def slot_copies(step):
        dest, where = partner(step)
        return (
            pltpu.make_async_remote_copy(
                src_ref=slots.at[dest], dst_ref=got_slots.at[me],
                send_sem=slot_send.at[step], recv_sem=slot_recv.at[step],
                device_id=where, device_id_type=MESH),
            pltpu.make_async_remote_copy(
                src_ref=aux.at[dest], dst_ref=got_aux.at[me],
                send_sem=aux_send.at[step], recv_sem=aux_recv.at[step],
                device_id=where, device_id_type=MESH),
        )

    def col_copy(step):
        dest = lax.rem(my_mem + step, mems)
        first = pl.multiple_of(dest * cols, LANES)
        return pltpu.make_async_remote_copy(
            src_ref=prior.at[:, :, pl.ds(first, cols)], dst_ref=fields.at[my_mem],
            send_sem=col_send.at[step], recv_sem=col_recv.at[step],
            device_id=(dest, my_patch), device_id_type=MESH)

    def start(step, carry):
        for copy in slot_copies(step):
            copy.start()
        return carry

    def finish(step, carry):
        for copy in slot_copies(step):
            copy.wait()
        return carry

    lax.fori_loop(1, devices, start, 0)
    for step in range(1, mems):
        col_copy(step).start()
    mine = (
        pltpu.make_async_copy(slots.at[me], got_slots.at[me], own_sem.at[0]),
        pltpu.make_async_copy(aux.at[me], got_aux.at[me], own_sem.at[1]),
        pltpu.make_async_copy(
            prior.at[:, :, pl.ds(pl.multiple_of(my_mem * cols, LANES), cols)],
            fields.at[my_mem], own_sem.at[2]),
    )
    for copy in mine:
        copy.start()
    for copy in mine:
        copy.wait()
    lax.fori_loop(1, devices, finish, 0)
    for step in range(1, mems):
        col_copy(step).wait()


def exchange(prior, slots, aux, mems, patches):
    part, lf, all_cols = prior.shape
    devices = mems * patches
    dma = pltpu.SemaphoreType.DMA
    return pl.pallas_call(
        functools.partial(exchange_kernel, mems, patches),
        out_shape=(
            jax.ShapeDtypeStruct((mems, part, lf, all_cols // mems), jnp.bfloat16),
            jax.ShapeDtypeStruct(slots.shape, slots.dtype),
            jax.ShapeDtypeStruct(aux.shape, aux.dtype),
        ),
        in_specs=[pl.BlockSpec(memory_space=pl.ANY)] * 3,
        out_specs=(pl.BlockSpec(memory_space=pl.ANY),) * 3,
        scratch_shapes=[dma((devices,)), dma((devices,)), dma((devices,)), dma((devices,)),
                        dma((mems,)), dma((mems,)), dma((3,))],
        compiler_params=pltpu.CompilerParams(collective_id=0, has_side_effects=True),
        name="exchange",
    )(prior, slots, aux)


def apply_kernel(mems, chunks, fields, weights, out, wide, mixed, buf, send, recv, own):
    my_mem, my_patch = lax.axis_index("mem"), lax.axis_index("patch")
    step = pl.program_id(0)
    part, lf, chunk = fields.shape[1], fields.shape[2], fields.shape[3]
    members = mems * part
    tiles = chunk // LANES
    cols = chunk * chunks
    half = LANES // 2

    @pl.when(step == 0)
    def _():
        barrier = pltpu.get_barrier_semaphore()
        for other in range(1, mems):
            pl.semaphore_signal(barrier, inc=1,
                                device_id=(lax.rem(my_mem + other, mems), my_patch),
                                device_id_type=MESH)
        pl.semaphore_wait(barrier, mems - 1)

    def place(owner, at):
        return out.at[:, :, pl.ds(pl.multiple_of(owner * cols + at * chunk, LANES), chunk)]

    def outgoing(at, other):
        dest = lax.rem(my_mem + other, mems)
        return pltpu.make_async_remote_copy(
            src_ref=buf.at[lax.rem(at, 2), dest], dst_ref=place(my_mem, at),
            send_sem=send.at[lax.rem(at, 2), other], recv_sem=recv.at[at, other],
            device_id=(dest, my_patch), device_id_type=MESH)

    def local_copy(at):
        return pltpu.make_async_copy(buf.at[lax.rem(at, 2), my_mem], place(my_mem, at),
                                     own.at[lax.rem(at, 2)])

    def drain(at):
        for other in range(1, mems):
            outgoing(at, other).wait_send()
        local_copy(at).wait()

    @pl.when(step >= 2)
    def _():
        drain(step - 2)

    for k in range(members):
        row = fields[k // part, k % part].astype(jnp.float32)
        for t in range(tiles):
            wide[t, lf * k:lf * k + lf, :] = row[:, t * LANES:(t + 1) * LANES]
    lane = lax.broadcasted_iota(jnp.int32, (members, LANES), 1)
    for t in range(tiles):
        averages, devs = [], []
        for f in range(lf):
            x = wide[t, pl.ds(f, members, stride=lf), :]
            average = jnp.sum(x, axis=0, keepdims=True) / members
            averages.append(average)
            devs.append((x - average).astype(jnp.bfloat16))
        y = jnp.dot(weights[t], jnp.concatenate(devs, axis=1), preferred_element_type=jnp.float32)
        for f in range(lf):
            z = y[:, f * LANES:(f + 1) * LANES]
            mixed[t, pl.ds(f, members, stride=lf), :] = averages[f] + jnp.where(
                lane < half, z[:members], z[members:])
    slot = lax.rem(step, 2)
    for j in range(members):
        row = jnp.concatenate([mixed[t, lf * j:lf * j + lf, :] for t in range(tiles)], axis=1)
        buf[slot, j // part, j % part] = row.astype(jnp.bfloat16)
    for other in range(1, mems):
        outgoing(step, other).start()
    local_copy(step).start()

    @pl.when(step == chunks - 1)
    def _():
        if chunks > 1:
            drain(step - 1)
        drain(step)

        def arrive(at, carry):
            for other in range(1, mems):
                outgoing(at, other).wait_recv()
            return carry

        lax.fori_loop(0, chunks, arrive, 0)


def apply_return(fields, weights, mems):
    unused, part, lf, cols = fields.shape
    members = mems * part
    chunk = CHUNK
    chunks = cols // chunk
    tiles = chunk // LANES
    dma = pltpu.SemaphoreType.DMA
    return pl.pallas_call(
        functools.partial(apply_kernel, mems, chunks),
        grid=(chunks,),
        out_shape=jax.ShapeDtypeStruct((part, lf, cols * mems), jnp.bfloat16),
        in_specs=[
            pl.BlockSpec((mems, part, lf, chunk), lambda i: (0, 0, 0, i)),
            pl.BlockSpec((tiles, 2 * members, members), lambda i: (i, 0, 0)),
        ],
        out_specs=pl.BlockSpec(memory_space=pl.ANY),
        scratch_shapes=[
            pltpu.VMEM((tiles, members * lf, LANES), jnp.float32),
            pltpu.VMEM((tiles, members * lf, LANES), jnp.float32),
            pltpu.VMEM((2, mems, part, lf, chunk), jnp.bfloat16),
            dma((2, mems)), dma((chunks, mems)), dma((2,)),
        ],
        compiler_params=pltpu.CompilerParams(collective_id=1, has_side_effects=True,
                                             vmem_limit_bytes=32 * 1024 * 1024),
        name="apply_return",
    )(fields, weights)


def local(prior, obs_prior, obs_depart, obs_rinv, loc_class, block_owner, block_patch):
    mems = lax.axis_size("mem")
    patches = lax.axis_size("patch")
    devices = mems * patches
    block_count, members, obs_count = obs_prior.shape
    capacity = 2 * block_count // devices
    slot_index = slot_positions(block_owner, devices, capacity)
    total = devices * capacity
    taper = 1.0 - loc_class.astype(jnp.float32) * 0.0625
    taper = (taper * taper).astype(jnp.bfloat16)
    tag = jnp.broadcast_to((block_patch + 1).astype(jnp.bfloat16)[:, None], obs_depart.shape)
    packed = jnp.stack([obs_depart, obs_rinv, taper, tag], axis=1)
    place = (slot_index[None, :] == jnp.arange(total, dtype=jnp.int32)[:, None])
    aux = jnp.einsum("sb,bro->sro", place.astype(jnp.bfloat16), packed,
                     preferred_element_type=jnp.float32).astype(jnp.bfloat16)
    slots = spread_blocks(slot_index, obs_prior, total)
    fields, got_slots, got_aux = exchange(
        prior,
        slots.reshape(devices, capacity, members, obs_count),
        aux.reshape(devices, capacity, 4, obs_count),
        mems, patches)
    side = got_aux.reshape(total, 4, obs_count)
    values = got_slots.reshape(total, members, obs_count)
    depart = side[:, 0]
    factor = side[:, 1].astype(jnp.float32) * side[:, 2].astype(jnp.float32)
    patch_of = side[:, 3, 0].astype(jnp.float32)
    average = jnp.sum(values, axis=1, keepdims=True, dtype=jnp.float32) / members
    deviation = (values.astype(jnp.float32) - average).astype(jnp.bfloat16)
    scaled = (deviation.astype(jnp.float32) * factor[:, None, :]).astype(jnp.bfloat16)
    gram_blocks = jnp.einsum("bko,bjo->bkj", scaled, deviation, preferred_element_type=jnp.float32)
    drive_blocks = jnp.einsum("bko,bo->bk", scaled, depart, preferred_element_type=jnp.float32)
    select = (patch_of[:, None] == (jnp.arange(PD, dtype=jnp.float32) + 1.0)[None, :]).astype(
        jnp.float32)
    gram = jnp.einsum("sp,skj->pkj", select, gram_blocks, precision=lax.Precision.HIGHEST)
    drive = jnp.einsum("sp,sk->pk", select, drive_blocks, precision=lax.Precision.HIGHEST)
    weights = jnp.swapaxes(analysis_weights(gram, drive), 1, 2)
    gathered = gather_weights(weights, patches)
    gathered = gathered.reshape(patches * PD // 2, 2 * members, members)
    return apply_return(fields, gathered, mems)


def solution(mesh):
    return jax.shard_map(
        local,
        mesh=mesh,
        in_specs=(
            P("mem", "patch", None),
            P(("mem", "patch"), None, None),
            P(("mem", "patch"), None),
            P(("mem", "patch"), None),
            P(("mem", "patch"), None),
            P(("mem", "patch"), None),
            P(("mem", "patch")),
        ),
        out_specs=P("mem", "patch", None),
        check_vma=False,
    )
```

```python
import functools
import jax
import jax.numpy as jnp
from jax import lax
from jax.experimental import pallas as pl
from jax.experimental.pallas import tpu as pltpu
from jax.sharding import PartitionSpec as P

PD = 16
ITERS = 10
LANES = 128
CHUNK = 512
MESH = pl.DeviceIdType.MESH


def batch_product(left, right):
    return jnp.einsum("pij,pjk->pik", left, right, precision=lax.Precision.HIGHEST)


def batch_apply(left, vector):
    return jnp.einsum("pij,pj->pi", left, vector, precision=lax.Precision.HIGHEST)


def analysis_weights(gram, drive_vec):
    members = gram.shape[1]
    identity = jnp.eye(members, dtype=jnp.float32)
    system = (members - 1.0) * identity + gram
    frobenius = jnp.sqrt(jnp.sum(system * system, axis=(1, 2)))
    scaled_sys = system / frobenius[:, None, None]
    inverse_root = 1.5 * identity - 0.5 * scaled_sys
    scaled_sys = batch_product(scaled_sys, inverse_root)
    for sweep_index in range(1, ITERS):
        correction = 1.5 * identity - 0.5 * batch_product(inverse_root, scaled_sys)
        scaled_sys = batch_product(scaled_sys, correction)
        inverse_root = batch_product(correction, inverse_root)
    root = inverse_root / jnp.sqrt(frobenius)[:, None, None]
    mean_weight = batch_apply(root, batch_apply(root, drive_vec))
    return (jnp.sqrt(members - 1.0) * root + mean_weight[:, :, None]).astype(jnp.bfloat16)


def slot_positions(block_owner, devices, capacity):
    block_dest = block_owner[:, 0]
    onehot = (block_dest[:, None] == jnp.arange(devices, dtype=jnp.int32)[None, :]).astype(
        jnp.int32
    )
    position = jnp.sum(jnp.cumsum(onehot, axis=0) * onehot, axis=1) - 1
    return block_dest * capacity + position


def spread_kernel(index, blocks, slots):
    slots[...] = jnp.zeros_like(slots)

    def place(b, carry):
        slots[index[b]] = blocks[b]
        return carry

    lax.fori_loop(0, blocks.shape[0], place, 0)


def spread_blocks(index, blocks, total):
    return pl.pallas_call(
        spread_kernel,
        out_shape=jax.ShapeDtypeStruct((total,) + blocks.shape[1:], blocks.dtype),
        in_specs=[pl.BlockSpec(memory_space=pltpu.SMEM), pl.BlockSpec(memory_space=pltpu.VMEM)],
        out_specs=pl.BlockSpec(memory_space=pltpu.VMEM),
        compiler_params=pltpu.CompilerParams(vmem_limit_bytes=32 * 1024 * 1024),
        name="spread_blocks",
    )(index, blocks)


def gather_kernel(mems, patches, mine, prior, out, fields, far_send, far_recv, near_send,
                  near_recv, col_send, col_recv, own_sem):
    my_mem, my_patch = lax.axis_index("mem"), lax.axis_index("patch")
    chips = patches // 2
    chip, core = my_patch // 2, lax.rem(my_patch, 2)
    sibling = (my_mem, chip * 2 + 1 - core)

    def peer(step):
        return lax.rem(chip + step, chips) * 2 + core

    barrier = pltpu.get_barrier_semaphore()
    pl.semaphore_signal(barrier, inc=1, device_id=sibling, device_id_type=MESH)
    for step in range(1, chips):
        pl.semaphore_signal(barrier, inc=1, device_id=(my_mem, peer(step)), device_id_type=MESH)
    for step in range(1, mems):
        pl.semaphore_signal(barrier, inc=1, device_id=(lax.rem(my_mem + step, mems), my_patch),
                            device_id_type=MESH)
    pl.semaphore_wait(barrier, chips + mems - 1)
    late, cols = fields.shape[1], fields.shape[-1]
    first_late = prior.shape[0] - late

    def piece(owner):
        return prior.at[pl.ds(first_late, late), :,
                        pl.ds(pl.multiple_of(owner * cols, LANES), cols)]

    def col_copy(step):
        dest = lax.rem(my_mem + step, mems)
        return pltpu.make_async_remote_copy(
            src_ref=piece(dest), dst_ref=fields.at[my_mem],
            send_sem=col_send.at[step], recv_sem=col_recv.at[step],
            device_id=(dest, my_patch), device_id_type=MESH)

    def far(step):
        return pltpu.make_async_remote_copy(
            src_ref=mine, dst_ref=out.at[my_patch],
            send_sem=far_send.at[step], recv_sem=far_recv.at[step],
            device_id=(my_mem, peer(step)), device_id_type=MESH)

    def near(step):
        source = mine if step == 0 else out.at[peer(chips - step)]
        return pltpu.make_async_remote_copy(
            src_ref=source, dst_ref=out.at[peer(chips - step)],
            send_sem=near_send.at[step], recv_sem=near_recv.at[step],
            device_id=sibling, device_id_type=MESH)

    for step in range(1, chips):
        far(step).start()
    near(0).start()
    for step in range(1, mems):
        col_copy(step).start()
    own = pltpu.make_async_copy(mine, out.at[my_patch], own_sem.at[0])
    own.start()
    kept = pltpu.make_async_copy(piece(my_mem), fields.at[my_mem], own_sem.at[1])
    kept.start()
    for step in range(1, chips):
        far(step).wait_recv()
        near(step).start()
    own.wait()
    kept.wait()
    for step in range(1, mems):
        col_copy(step).wait()
    for step in range(1, chips):
        far(step).wait_send()
    for step in range(chips):
        near(step).wait()


def gather_weights(weights, prior, mems, patches):
    dma = pltpu.SemaphoreType.DMA
    chips = patches // 2
    part, lf, all_cols = prior.shape
    return pl.pallas_call(
        functools.partial(gather_kernel, mems, patches),
        out_shape=(
            jax.ShapeDtypeStruct((patches,) + weights.shape, weights.dtype),
            jax.ShapeDtypeStruct((mems, part - part // 2, lf, all_cols // mems), prior.dtype),
        ),
        in_specs=[pl.BlockSpec(memory_space=pltpu.VMEM), pl.BlockSpec(memory_space=pl.ANY)],
        out_specs=(pl.BlockSpec(memory_space=pl.ANY),) * 2,
        scratch_shapes=[dma((chips,)), dma((chips,)), dma((chips,)), dma((chips,)),
                        dma((mems,)), dma((mems,)), dma((2,))],
        compiler_params=pltpu.CompilerParams(collective_id=2, has_side_effects=True),
        name="gather_weights",
    )(weights, prior)


def exchange_kernel(mems, patches, prior, slots, aux, fields, got_slots, got_aux,
                    slot_send, slot_recv, aux_send, aux_recv, col_send, col_recv, own_sem):
    my_mem, my_patch = lax.axis_index("mem"), lax.axis_index("patch")
    devices = mems * patches
    me = my_mem * patches + my_patch
    early, cols = fields.shape[1], fields.shape[-1]

    def partner(step):
        dest = lax.rem(me + step, devices)
        return dest, (dest // patches, lax.rem(dest, patches))

    barrier = pltpu.get_barrier_semaphore()

    def greet(step, carry):
        pl.semaphore_signal(barrier, inc=1, device_id=partner(step)[1], device_id_type=MESH)
        return carry

    lax.fori_loop(1, devices, greet, 0)
    pl.semaphore_wait(barrier, devices - 1)

    def slot_copies(step):
        dest, where = partner(step)
        return (
            pltpu.make_async_remote_copy(
                src_ref=slots.at[dest], dst_ref=got_slots.at[me],
                send_sem=slot_send.at[step], recv_sem=slot_recv.at[step],
                device_id=where, device_id_type=MESH),
            pltpu.make_async_remote_copy(
                src_ref=aux.at[dest], dst_ref=got_aux.at[me],
                send_sem=aux_send.at[step], recv_sem=aux_recv.at[step],
                device_id=where, device_id_type=MESH),
        )

    def col_copy(step):
        dest = lax.rem(my_mem + step, mems)
        first = pl.multiple_of(dest * cols, LANES)
        return pltpu.make_async_remote_copy(
            src_ref=prior.at[pl.ds(0, early), :, pl.ds(first, cols)], dst_ref=fields.at[my_mem],
            send_sem=col_send.at[step], recv_sem=col_recv.at[step],
            device_id=(dest, my_patch), device_id_type=MESH)

    def start(step, carry):
        for copy in slot_copies(step):
            copy.start()
        return carry

    def finish(step, carry):
        for copy in slot_copies(step):
            copy.wait()
        return carry

    lax.fori_loop(1, devices, start, 0)
    for step in range(1, mems):
        col_copy(step).start()
    mine = (
        pltpu.make_async_copy(slots.at[me], got_slots.at[me], own_sem.at[0]),
        pltpu.make_async_copy(aux.at[me], got_aux.at[me], own_sem.at[1]),
        pltpu.make_async_copy(
            prior.at[pl.ds(0, early), :, pl.ds(pl.multiple_of(my_mem * cols, LANES), cols)],
            fields.at[my_mem], own_sem.at[2]),
    )
    for copy in mine:
        copy.start()
    for copy in mine:
        copy.wait()
    lax.fori_loop(1, devices, finish, 0)
    for step in range(1, mems):
        col_copy(step).wait()


def exchange(prior, slots, aux, mems, patches):
    part, lf, all_cols = prior.shape
    devices = mems * patches
    dma = pltpu.SemaphoreType.DMA
    return pl.pallas_call(
        functools.partial(exchange_kernel, mems, patches),
        out_shape=(
            jax.ShapeDtypeStruct((mems, part // 2, lf, all_cols // mems), jnp.bfloat16),
            jax.ShapeDtypeStruct(slots.shape, slots.dtype),
            jax.ShapeDtypeStruct(aux.shape, aux.dtype),
        ),
        in_specs=[pl.BlockSpec(memory_space=pl.ANY)] * 3,
        out_specs=(pl.BlockSpec(memory_space=pl.ANY),) * 3,
        scratch_shapes=[dma((devices,)), dma((devices,)), dma((devices,)), dma((devices,)),
                        dma((mems,)), dma((mems,)), dma((3,))],
        compiler_params=pltpu.CompilerParams(collective_id=0, has_side_effects=True),
        name="exchange",
    )(prior, slots, aux)


def apply_kernel(mems, chunks, early, late, weights, out, wide, mixed, buf, send, recv, own):
    my_mem, my_patch = lax.axis_index("mem"), lax.axis_index("patch")
    step = pl.program_id(0)
    split, lf, chunk = early.shape[1], early.shape[2], early.shape[3]
    part = split + late.shape[1]
    members = mems * part
    tiles = chunk // LANES
    cols = chunk * chunks
    half = LANES // 2
    group = LANES // (2 * tiles)

    @pl.when(step == 0)
    def _():
        barrier = pltpu.get_barrier_semaphore()
        for other in range(1, mems):
            pl.semaphore_signal(barrier, inc=1,
                                device_id=(lax.rem(my_mem + other, mems), my_patch),
                                device_id_type=MESH)
        pl.semaphore_wait(barrier, mems - 1)

    def place(owner, at):
        return out.at[:, :, pl.ds(pl.multiple_of(owner * cols + at * chunk, LANES), chunk)]

    def outgoing(at, other):
        dest = lax.rem(my_mem + other, mems)
        return pltpu.make_async_remote_copy(
            src_ref=buf.at[lax.rem(at, 2), dest], dst_ref=place(my_mem, at),
            send_sem=send.at[lax.rem(at, 2), other], recv_sem=recv.at[at, other],
            device_id=(dest, my_patch), device_id_type=MESH)

    def local_copy(at):
        return pltpu.make_async_copy(buf.at[lax.rem(at, 2), my_mem], place(my_mem, at),
                                     own.at[lax.rem(at, 2)])

    def drain(at):
        for other in range(1, mems):
            outgoing(at, other).wait_send()
        local_copy(at).wait()

    @pl.when(step >= 2)
    def _():
        drain(step - 2)

    for k in range(members):
        source, at = divmod(k, part)
        row = early[source, at] if at < split else late[source, at - split]
        row = row.astype(jnp.float32)
        for t in range(tiles):
            wide[t, lf * k:lf * k + lf, :] = row[:, t * LANES:(t + 1) * LANES]
    lane = lax.broadcasted_iota(jnp.int32, (members, LANES), 1)
    for t in range(tiles):
        averages, devs = [], []
        for f in range(lf):
            x = wide[t, pl.ds(f, members, stride=lf), :]
            average = jnp.sum(x, axis=0, keepdims=True) / members
            averages.append(average)
            devs.append((x - average).astype(jnp.bfloat16))
        pair = []
        for p in (2 * t, 2 * t + 1):
            pair.append(jnp.concatenate(
                [weights[g, :, p * group:(p + 1) * group] for g in range(members // group)],
                axis=1))
        y = jnp.dot(jnp.concatenate(pair, axis=0), jnp.concatenate(devs, axis=1), preferred_element_type=jnp.float32)
        for f in range(lf):
            z = y[:, f * LANES:(f + 1) * LANES]
            mixed[t, pl.ds(f, members, stride=lf), :] = averages[f] + jnp.where(
                lane < half, z[:members], z[members:])
    slot = lax.rem(step, 2)
    for j in range(members):
        row = jnp.concatenate([mixed[t, lf * j:lf * j + lf, :] for t in range(tiles)], axis=1)
        buf[slot, j // part, j % part] = row.astype(jnp.bfloat16)
    for other in range(1, mems):
        outgoing(step, other).start()
    local_copy(step).start()

    @pl.when(step == chunks - 1)
    def _():
        if chunks > 1:
            drain(step - 1)
        drain(step)

        def arrive(at, carry):
            for other in range(1, mems):
                outgoing(at, other).wait_recv()
            return carry

        lax.fori_loop(0, chunks, arrive, 0)


def apply_return(early, late, weights, mems):
    unused, split, lf, cols = early.shape
    rest = late.shape[1]
    part = split + rest
    members = mems * part
    chunk = CHUNK
    chunks = cols // chunk
    tiles = chunk // LANES
    dma = pltpu.SemaphoreType.DMA
    return pl.pallas_call(
        functools.partial(apply_kernel, mems, chunks),
        grid=(chunks,),
        out_shape=jax.ShapeDtypeStruct((part, lf, cols * mems), jnp.bfloat16),
        in_specs=[
            pl.BlockSpec((mems, split, lf, chunk), lambda i: (0, 0, 0, i)),
            pl.BlockSpec((mems, rest, lf, chunk), lambda i: (0, 0, 0, i)),
            pl.BlockSpec((None,) + weights.shape[1:], lambda i: (i, 0, 0, 0)),
        ],
        out_specs=pl.BlockSpec(memory_space=pl.ANY),
        scratch_shapes=[
            pltpu.VMEM((tiles, members * lf, LANES), jnp.float32),
            pltpu.VMEM((tiles, members * lf, LANES), jnp.float32),
            pltpu.VMEM((2, mems, part, lf, chunk), jnp.bfloat16),
            dma((2, mems)), dma((chunks, mems)), dma((2,)),
        ],
        compiler_params=pltpu.CompilerParams(collective_id=1, has_side_effects=True,
                                             vmem_limit_bytes=32 * 1024 * 1024),
        name="apply_return",
    )(early, late, weights)


def local(prior, obs_prior, obs_depart, obs_rinv, loc_class, block_owner, block_patch):
    mems = lax.axis_size("mem")
    patches = lax.axis_size("patch")
    devices = mems * patches
    block_count, members, obs_count = obs_prior.shape
    capacity = 2 * block_count // devices
    slot_index = slot_positions(block_owner, devices, capacity)
    total = devices * capacity
    taper = 1.0 - loc_class.astype(jnp.float32) * 0.0625
    taper = (taper * taper).astype(jnp.bfloat16)
    tag = jnp.broadcast_to((block_patch + 1).astype(jnp.bfloat16)[:, None], obs_depart.shape)
    packed = jnp.stack([obs_depart, obs_rinv, taper, tag], axis=1)
    place = (slot_index[None, :] == jnp.arange(total, dtype=jnp.int32)[:, None])
    aux = jnp.einsum("sb,bro->sro", place.astype(jnp.bfloat16), packed,
                     preferred_element_type=jnp.float32).astype(jnp.bfloat16)
    slots = spread_blocks(slot_index, obs_prior, total)
    fields, got_slots, got_aux = exchange(
        prior,
        slots.reshape(devices, capacity, members, obs_count),
        aux.reshape(devices, capacity, 4, obs_count),
        mems, patches)
    side = got_aux.reshape(total, 4, obs_count)
    values = got_slots.reshape(total, members, obs_count)
    depart = side[:, 0]
    factor = side[:, 1].astype(jnp.float32) * side[:, 2].astype(jnp.float32)
    patch_of = side[:, 3, 0].astype(jnp.float32)
    average = jnp.sum(values, axis=1, keepdims=True, dtype=jnp.float32) / members
    deviation = (values.astype(jnp.float32) - average).astype(jnp.bfloat16)
    scaled = (deviation.astype(jnp.float32) * factor[:, None, :]).astype(jnp.bfloat16)
    gram_blocks = jnp.einsum("bko,bjo->bkj", scaled, deviation, preferred_element_type=jnp.float32)
    drive_blocks = jnp.einsum("bko,bo->bk", scaled, depart, preferred_element_type=jnp.float32)
    select = (patch_of[:, None] == (jnp.arange(PD, dtype=jnp.float32) + 1.0)[None, :]).astype(
        jnp.float32)
    gram = jnp.einsum("sp,skj->pkj", select, gram_blocks, precision=lax.Precision.HIGHEST)
    drive = jnp.einsum("sp,sk->pk", select, drive_blocks, precision=lax.Precision.HIGHEST)
    weights = jnp.swapaxes(analysis_weights(gram, drive), 1, 2)
    per = CHUNK // LANES * 2
    group = LANES // per
    weights = weights.reshape(PD // per, per, members, members // group, group)
    weights = weights.transpose(0, 3, 2, 1, 4).reshape(
        PD // per, members // group, members, LANES)
    gathered, late = gather_weights(weights, prior, mems, patches)
    gathered = gathered.reshape((patches * PD // per,) + gathered.shape[2:])
    return apply_return(fields, late, gathered, mems)


def solution(mesh):
    return jax.shard_map(
        local,
        mesh=mesh,
        in_specs=(
            P("mem", "patch", None),
            P(("mem", "patch"), None, None),
            P(("mem", "patch"), None),
            P(("mem", "patch"), None),
            P(("mem", "patch"), None),
            P(("mem", "patch"), None),
            P(("mem", "patch")),
        ),
        out_specs=P("mem", "patch", None),
        check_vma=False,
    )
```

```python
import functools
import jax
import jax.numpy as jnp
from jax import lax
from jax.experimental import pallas as pl
from jax.experimental.pallas import tpu as pltpu
from jax.sharding import PartitionSpec as P

PD = 16
ITERS = 10
LANES = 128
CHUNK = 512
MESH = pl.DeviceIdType.MESH


def batch_product(left, right):
    return jnp.einsum("pij,pjk->pik", left, right, precision=lax.Precision.HIGHEST)


def batch_apply(left, vector):
    return jnp.einsum("pij,pj->pi", left, vector, precision=lax.Precision.HIGHEST)


def analysis_weights(gram, drive_vec):
    members = gram.shape[1]
    identity = jnp.eye(members, dtype=jnp.float32)
    system = (members - 1.0) * identity + gram
    frobenius = jnp.sqrt(jnp.sum(system * system, axis=(1, 2)))
    scaled_sys = system / frobenius[:, None, None]
    inverse_root = 1.5 * identity - 0.5 * scaled_sys
    scaled_sys = batch_product(scaled_sys, inverse_root)
    for sweep_index in range(1, ITERS):
        correction = 1.5 * identity - 0.5 * batch_product(inverse_root, scaled_sys)
        scaled_sys = batch_product(scaled_sys, correction)
        inverse_root = batch_product(correction, inverse_root)
    root = inverse_root / jnp.sqrt(frobenius)[:, None, None]
    mean_weight = batch_apply(root, batch_apply(root, drive_vec))
    return (jnp.sqrt(members - 1.0) * root + mean_weight[:, :, None]).astype(jnp.bfloat16)


def slot_positions(block_owner, devices, capacity):
    block_dest = block_owner[:, 0]
    onehot = (block_dest[:, None] == jnp.arange(devices, dtype=jnp.int32)[None, :]).astype(
        jnp.int32
    )
    position = jnp.sum(jnp.cumsum(onehot, axis=0) * onehot, axis=1) - 1
    return block_dest * capacity + position


def gram_kernel(index, tags, blocks, factor, depart, slots):
    slots[...] = jnp.zeros_like(slots)
    members = blocks.shape[1]
    lane = lax.broadcasted_iota(jnp.int32, (16, 16), 1)

    def group(at, carry):
        first = pl.multiple_of(at * 8, 8)
        factors = factor[pl.ds(first, 8), :]
        departs = depart[pl.ds(first, 8), :]
        for i in range(8):
            b = first + i
            x = blocks[b].astype(jnp.float32)
            average = jnp.sum(x, axis=0, keepdims=True) / members
            deviation = (x - average).astype(jnp.bfloat16)
            scaled = (deviation.astype(jnp.float32) * factors[i:i + 1]).astype(jnp.bfloat16)
            g = lax.dot_general(scaled, deviation, (((1,), (1,)), ((), ())),
                                preferred_element_type=jnp.float32)
            drive = jnp.sum(scaled.astype(jnp.float32) * departs[i:i + 1], axis=1, keepdims=True)
            extra = jnp.full((16, 16), tags[b], jnp.float32)
            for q in range(5):
                extra = jnp.where(lane == q, drive[16 * q:16 * q + 16], extra)
            top = jnp.concatenate(
                [g[48:64, 48:64], g[:16, :16], g[48:64, :48], g[16:32, :32], extra], axis=1)
            low = jnp.concatenate([g[64:80, 48:80], g[64:80, :48], g[32:48, :48]], axis=1)
            slots[index[b]] = jnp.concatenate([top, low], axis=0)
        return carry

    lax.fori_loop(0, blocks.shape[0] // 8, group, 0)


def gram_slots(index, tags, blocks, factor, depart, total):
    vmem, smem = pltpu.VMEM, pltpu.SMEM
    return pl.pallas_call(
        gram_kernel,
        out_shape=jax.ShapeDtypeStruct((total, 32, LANES), jnp.float32),
        in_specs=[pl.BlockSpec(memory_space=m) for m in (smem, smem, vmem, vmem, vmem)],
        out_specs=pl.BlockSpec(memory_space=pltpu.VMEM),
        compiler_params=pltpu.CompilerParams(vmem_limit_bytes=32 * 1024 * 1024),
        name="gram_slots",
    )(index, tags, blocks, factor, depart)


def flip(block):
    return jnp.swapaxes(block, 1, 2)


def unpack_gram(packed):
    top, low = packed[:, :16], packed[:, 16:]
    third, second = packed[:, :, 32:80], packed[:, :, 80:96]

    def square(first, corner, last):
        return jnp.concatenate([jnp.concatenate([first, flip(corner)], axis=2),
                                jnp.concatenate([corner, last], axis=2)], axis=1)

    mid = square(top[:, :, 96:112], low[:, :, 96:112], low[:, :, 112:128])
    end = square(top[:, :, :16], low[:, :, :16], low[:, :, 16:32])
    across = flip(third)
    gram = jnp.concatenate([
        jnp.concatenate([top[:, :, 16:32], flip(second), across[:, :16]], axis=2),
        jnp.concatenate([second, mid, across[:, 16:]], axis=2),
        jnp.concatenate([third, end], axis=2)], axis=1)
    drive = jnp.concatenate([top[:, :, 112 + q] for q in range(5)], axis=1)
    return gram, drive


def gather_kernel(mems, patches, mine, prior, out, fields, far_send, far_recv, near_send,
                  near_recv, col_send, col_recv, own_sem):
    my_mem, my_patch = lax.axis_index("mem"), lax.axis_index("patch")
    chips = patches // 2
    chip, core = my_patch // 2, lax.rem(my_patch, 2)
    sibling = (my_mem, chip * 2 + 1 - core)

    def peer(step):
        return lax.rem(chip + step, chips) * 2 + core

    barrier = pltpu.get_barrier_semaphore()
    pl.semaphore_signal(barrier, inc=1, device_id=sibling, device_id_type=MESH)
    for step in range(1, chips):
        pl.semaphore_signal(barrier, inc=1, device_id=(my_mem, peer(step)), device_id_type=MESH)
    for step in range(1, mems):
        pl.semaphore_signal(barrier, inc=1, device_id=(lax.rem(my_mem + step, mems), my_patch),
                            device_id_type=MESH)
    pl.semaphore_wait(barrier, chips + mems - 1)
    late, cols = fields.shape[1], fields.shape[-1]
    first_late = prior.shape[0] - late

    def piece(owner):
        return prior.at[pl.ds(first_late, late), :,
                        pl.ds(pl.multiple_of(owner * cols, LANES), cols)]

    def col_copy(step):
        dest = lax.rem(my_mem + step, mems)
        return pltpu.make_async_remote_copy(
            src_ref=piece(dest), dst_ref=fields.at[my_mem],
            send_sem=col_send.at[step], recv_sem=col_recv.at[step],
            device_id=(dest, my_patch), device_id_type=MESH)

    def far(step):
        return pltpu.make_async_remote_copy(
            src_ref=mine, dst_ref=out.at[my_patch],
            send_sem=far_send.at[step], recv_sem=far_recv.at[step],
            device_id=(my_mem, peer(step)), device_id_type=MESH)

    def near(step):
        source = mine if step == 0 else out.at[peer(chips - step)]
        return pltpu.make_async_remote_copy(
            src_ref=source, dst_ref=out.at[peer(chips - step)],
            send_sem=near_send.at[step], recv_sem=near_recv.at[step],
            device_id=sibling, device_id_type=MESH)

    for step in range(1, chips):
        far(step).start()
    near(0).start()
    for step in range(1, mems):
        col_copy(step).start()
    own = pltpu.make_async_copy(mine, out.at[my_patch], own_sem.at[0])
    own.start()
    kept = pltpu.make_async_copy(piece(my_mem), fields.at[my_mem], own_sem.at[1])
    kept.start()
    for step in range(1, chips):
        far(step).wait_recv()
        near(step).start()
    own.wait()
    kept.wait()
    for step in range(1, mems):
        col_copy(step).wait()
    for step in range(1, chips):
        far(step).wait_send()
    for step in range(chips):
        near(step).wait()


def gather_weights(weights, prior, mems, patches):
    dma = pltpu.SemaphoreType.DMA
    chips = patches // 2
    part, lf, all_cols = prior.shape
    return pl.pallas_call(
        functools.partial(gather_kernel, mems, patches),
        out_shape=(
            jax.ShapeDtypeStruct((patches,) + weights.shape, weights.dtype),
            jax.ShapeDtypeStruct((mems, part - part // 2, lf, all_cols // mems), prior.dtype),
        ),
        in_specs=[pl.BlockSpec(memory_space=pltpu.VMEM), pl.BlockSpec(memory_space=pl.ANY)],
        out_specs=(pl.BlockSpec(memory_space=pl.ANY),) * 2,
        scratch_shapes=[dma((chips,)), dma((chips,)), dma((chips,)), dma((chips,)),
                        dma((mems,)), dma((mems,)), dma((2,))],
        compiler_params=pltpu.CompilerParams(collective_id=2, has_side_effects=True),
        name="gather_weights",
    )(weights, prior)


def exchange_kernel(mems, patches, prior, slots, fields, got_slots,
                    slot_send, slot_recv, col_send, col_recv, own_sem):
    my_mem, my_patch = lax.axis_index("mem"), lax.axis_index("patch")
    devices = mems * patches
    me = my_mem * patches + my_patch
    early, cols = fields.shape[1], fields.shape[-1]

    def partner(step):
        dest = lax.rem(me + step, devices)
        return dest, (dest // patches, lax.rem(dest, patches))

    barrier = pltpu.get_barrier_semaphore()

    def greet(step, carry):
        pl.semaphore_signal(barrier, inc=1, device_id=partner(step)[1], device_id_type=MESH)
        return carry

    lax.fori_loop(1, devices, greet, 0)
    pl.semaphore_wait(barrier, devices - 1)

    def slot_copies(step):
        dest, where = partner(step)
        return (
            pltpu.make_async_remote_copy(
                src_ref=slots.at[dest], dst_ref=got_slots.at[me],
                send_sem=slot_send.at[step], recv_sem=slot_recv.at[step],
                device_id=where, device_id_type=MESH),
        )

    def col_copy(step):
        dest = lax.rem(my_mem + step, mems)
        first = pl.multiple_of(dest * cols, LANES)
        return pltpu.make_async_remote_copy(
            src_ref=prior.at[pl.ds(0, early), :, pl.ds(first, cols)], dst_ref=fields.at[my_mem],
            send_sem=col_send.at[step], recv_sem=col_recv.at[step],
            device_id=(dest, my_patch), device_id_type=MESH)

    def start(step, carry):
        for copy in slot_copies(step):
            copy.start()
        return carry

    def finish(step, carry):
        for copy in slot_copies(step):
            copy.wait()
        return carry

    lax.fori_loop(1, devices, start, 0)
    for step in range(1, mems):
        col_copy(step).start()
    mine = (
        pltpu.make_async_copy(slots.at[me], got_slots.at[me], own_sem.at[0]),
        pltpu.make_async_copy(
            prior.at[pl.ds(0, early), :, pl.ds(pl.multiple_of(my_mem * cols, LANES), cols)],
            fields.at[my_mem], own_sem.at[2]),
    )
    for copy in mine:
        copy.start()
    for copy in mine:
        copy.wait()
    lax.fori_loop(1, devices, finish, 0)
    for step in range(1, mems):
        col_copy(step).wait()


def exchange(prior, slots, mems, patches):
    part, lf, all_cols = prior.shape
    devices = mems * patches
    dma = pltpu.SemaphoreType.DMA
    return pl.pallas_call(
        functools.partial(exchange_kernel, mems, patches),
        out_shape=(
            jax.ShapeDtypeStruct((mems, part // 2, lf, all_cols // mems), jnp.bfloat16),
            jax.ShapeDtypeStruct(slots.shape, slots.dtype),
        ),
        in_specs=[pl.BlockSpec(memory_space=pl.ANY)] * 2,
        out_specs=(pl.BlockSpec(memory_space=pl.ANY),) * 2,
        scratch_shapes=[dma((devices,)), dma((devices,)), dma((mems,)), dma((mems,)), dma((3,))],
        compiler_params=pltpu.CompilerParams(collective_id=0, has_side_effects=True),
        name="exchange",
    )(prior, slots)


def apply_kernel(mems, chunks, early, late, weights, out, wide, mixed, buf, send, recv, own):
    my_mem, my_patch = lax.axis_index("mem"), lax.axis_index("patch")
    step = pl.program_id(0)
    split, lf, chunk = early.shape[1], early.shape[2], early.shape[3]
    part = split + late.shape[1]
    members = mems * part
    tiles = chunk // LANES
    cols = chunk * chunks
    half = LANES // 2
    group = LANES // (2 * tiles)

    @pl.when(step == 0)
    def _():
        barrier = pltpu.get_barrier_semaphore()
        for other in range(1, mems):
            pl.semaphore_signal(barrier, inc=1,
                                device_id=(lax.rem(my_mem + other, mems), my_patch),
                                device_id_type=MESH)
        pl.semaphore_wait(barrier, mems - 1)

    def place(owner, at):
        return out.at[:, :, pl.ds(pl.multiple_of(owner * cols + at * chunk, LANES), chunk)]

    def outgoing(at, other):
        dest = lax.rem(my_mem + other, mems)
        return pltpu.make_async_remote_copy(
            src_ref=buf.at[lax.rem(at, 2), dest], dst_ref=place(my_mem, at),
            send_sem=send.at[lax.rem(at, 2), other], recv_sem=recv.at[at, other],
            device_id=(dest, my_patch), device_id_type=MESH)

    def local_copy(at):
        return pltpu.make_async_copy(buf.at[lax.rem(at, 2), my_mem], place(my_mem, at),
                                     own.at[lax.rem(at, 2)])

    def drain(at):
        for other in range(1, mems):
            outgoing(at, other).wait_send()
        local_copy(at).wait()

    @pl.when(step >= 2)
    def _():
        drain(step - 2)

    for k in range(members):
        source, at = divmod(k, part)
        row = early[source, at] if at < split else late[source, at - split]
        row = row.astype(jnp.float32)
        for t in range(tiles):
            wide[t, lf * k:lf * k + lf, :] = row[:, t * LANES:(t + 1) * LANES]
    lane = lax.broadcasted_iota(jnp.int32, (members, LANES), 1)
    for t in range(tiles):
        averages, devs = [], []
        for f in range(lf):
            x = wide[t, pl.ds(f, members, stride=lf), :]
            average = jnp.sum(x, axis=0, keepdims=True) / members
            averages.append(average)
            devs.append((x - average).astype(jnp.bfloat16))
        pair = []
        for p in (2 * t, 2 * t + 1):
            pair.append(jnp.concatenate(
                [weights[g, :, p * group:(p + 1) * group] for g in range(members // group)],
                axis=1))
        y = jnp.dot(jnp.concatenate(pair, axis=0), jnp.concatenate(devs, axis=1), preferred_element_type=jnp.float32)
        for f in range(lf):
            z = y[:, f * LANES:(f + 1) * LANES]
            mixed[t, pl.ds(f, members, stride=lf), :] = averages[f] + jnp.where(
                lane < half, z[:members], z[members:])
    slot = lax.rem(step, 2)
    for j in range(members):
        row = jnp.concatenate([mixed[t, lf * j:lf * j + lf, :] for t in range(tiles)], axis=1)
        buf[slot, j // part, j % part] = row.astype(jnp.bfloat16)
    for other in range(1, mems):
        outgoing(step, other).start()
    local_copy(step).start()

    @pl.when(step == chunks - 1)
    def _():
        if chunks > 1:
            drain(step - 1)
        drain(step)

        def arrive(at, carry):
            for other in range(1, mems):
                outgoing(at, other).wait_recv()
            return carry

        lax.fori_loop(0, chunks, arrive, 0)


def apply_return(early, late, weights, mems):
    unused, split, lf, cols = early.shape
    rest = late.shape[1]
    part = split + rest
    members = mems * part
    chunk = CHUNK
    chunks = cols // chunk
    tiles = chunk // LANES
    dma = pltpu.SemaphoreType.DMA
    return pl.pallas_call(
        functools.partial(apply_kernel, mems, chunks),
        grid=(chunks,),
        out_shape=jax.ShapeDtypeStruct((part, lf, cols * mems), jnp.bfloat16),
        in_specs=[
            pl.BlockSpec((mems, split, lf, chunk), lambda i: (0, 0, 0, i)),
            pl.BlockSpec((mems, rest, lf, chunk), lambda i: (0, 0, 0, i)),
            pl.BlockSpec((None,) + weights.shape[1:], lambda i: (i, 0, 0, 0)),
        ],
        out_specs=pl.BlockSpec(memory_space=pl.ANY),
        scratch_shapes=[
            pltpu.VMEM((tiles, members * lf, LANES), jnp.float32),
            pltpu.VMEM((tiles, members * lf, LANES), jnp.float32),
            pltpu.VMEM((2, mems, part, lf, chunk), jnp.bfloat16),
            dma((2, mems)), dma((chunks, mems)), dma((2,)),
        ],
        compiler_params=pltpu.CompilerParams(collective_id=1, has_side_effects=True,
                                             vmem_limit_bytes=32 * 1024 * 1024),
        name="apply_return",
    )(early, late, weights)


def local(prior, obs_prior, obs_depart, obs_rinv, loc_class, block_owner, block_patch):
    mems = lax.axis_size("mem")
    patches = lax.axis_size("patch")
    devices = mems * patches
    block_count, members, obs_count = obs_prior.shape
    capacity = 2 * block_count // devices
    slot_index = slot_positions(block_owner, devices, capacity)
    total = devices * capacity
    taper = 1.0 - loc_class.astype(jnp.float32) * 0.0625
    factor = taper * taper * obs_rinv.astype(jnp.float32)
    tags = (block_patch + 1).astype(jnp.float32)
    slots = gram_slots(slot_index, tags, obs_prior, factor, obs_depart.astype(jnp.float32), total)
    fields, got = exchange(prior, slots.reshape(devices, capacity, 32, LANES), mems, patches)
    got = got.reshape(total, 32, LANES)
    select = (got[:, 0, LANES - 1][:, None] == (
        jnp.arange(PD, dtype=jnp.float32) + 1.0)[None, :]).astype(jnp.float32)
    gram, drive = unpack_gram(
        jnp.einsum("sp,srl->prl", select, got, precision=lax.Precision.HIGHEST))
    weights = jnp.swapaxes(analysis_weights(gram, drive), 1, 2)
    per = CHUNK // LANES * 2
    group = LANES // per
    weights = weights.reshape(PD // per, per, members, members // group, group)
    weights = weights.transpose(0, 3, 2, 1, 4).reshape(
        PD // per, members // group, members, LANES)
    gathered, late = gather_weights(weights, prior, mems, patches)
    gathered = gathered.reshape((patches * PD // per,) + gathered.shape[2:])
    return apply_return(fields, late, gathered, mems)


def solution(mesh):
    return jax.shard_map(
        local,
        mesh=mesh,
        in_specs=(
            P("mem", "patch", None),
            P(("mem", "patch"), None, None),
            P(("mem", "patch"), None),
            P(("mem", "patch"), None),
            P(("mem", "patch"), None),
            P(("mem", "patch"), None),
            P(("mem", "patch")),
        ),
        out_specs=P("mem", "patch", None),
        check_vma=False,
    )
```
